512 devices in a mesh: seq: 2 (over z_hi), ri: 16 (over y, core), rj: 16 (over z_lo, x).
Axes of the slice: x: 4, y: 8, z: 8 (z_hi: 2, z_lo: 4; z = z_hi * 4 + z_lo), core: 2. Of those that a mesh axis runs over, the one named last changes fastest.
Arguments:
- homolog_embedding: bfloat16 [512, 1024, 256], P('seq', ('ri', 'rj')), may hold values from -6 to 6
- standardizer_scaling: float32 [256], replicated, may hold values from 0.1 to 1.9
- standardizer_shift: float32 [256], replicated, may hold values from -3 to 3
- paired_projector_matrix: bfloat16 [256, 64], replicated, may hold values from -0.375 to 0.375
- final_projector_matrix: bfloat16 [1024, 128], replicated, may hold values from -4 to 4
- final_offset_vector: float32 [128], replicated, may hold values from -3 to 3
Outputs:
- pair_update: bfloat16 [1024, 1024, 128], P(('ri', 'seq'), 'rj')
The draws below stay inside these ranges and needn't reach their ends.
All inputs are finite; a program needn't handle non-finite values.
Results may differ from the reference program's by a relative error of at most 0.0049.
Values may be sent and summed in bfloat16 or wider, within the bound.
A program may use at most 64 MiB of HBM per device.

```python
import jax
import jax.numpy as jnp
from jax import lax

FEATURE_DEPTH_M = 256
CP = 32
CZ = 128
SEQ_DEV = 256
HOMOLOG_ROWS = 512
CHAIN_POSITIONS = 1024
N_SEQ = 2


def levels(key, extent, pieces, smallest, top_value):
    factor_of, own = 1.0, jax.random.fold_in(key, 6)
    for position, blocks in pieces:
        steps = jnp.exp(jax.random.uniform(jax.random.fold_in(own, position), (blocks,), jnp.float32, smallest / len(pieces), top_value / len(pieces)))
        factor_of = factor_of * jnp.repeat(steps, extent[position] // blocks).reshape([-1 if axis == position else 1 for axis in range(len(extent))])
    return factor_of


def centred(stream_key, dims, width, reach, pieces=(), held_as=jnp.bfloat16):
    values = jax.random.normal(stream_key, dims, jnp.float32) * width
    if len(pieces) > 0:
        values = levels(stream_key, dims, pieces, -0.22, 0.18) * values
    return jnp.clip(values, min=-reach, max=reach).astype(held_as)


def setup_inputs(seed: int = 0) -> dict:
    key_list = jax.random.split(jax.random.key(seed), 7)
    homolog_embedding = centred(key_list[0], (HOMOLOG_ROWS, CHAIN_POSITIONS, FEATURE_DEPTH_M), 1.0, 6.0, ((0, 2), (1, 256)))
    standardizer_scaling = jnp.clip(1.0 + 0.18 * jax.random.normal(key_list[1], (FEATURE_DEPTH_M,), jnp.float32), 0.1, 1.9)
    standardizer_shift = centred(key_list[2], (FEATURE_DEPTH_M,), 0.5, 3.0, (), jnp.float32)
    paired_projector_matrix = centred(key_list[3], (FEATURE_DEPTH_M, 2 * CP), FEATURE_DEPTH_M ** -0.5, 0.375)
    final_projector_matrix = centred(key_list[4], (CP * CP, CZ), (CP * CP // (N_SEQ * SEQ_DEV)) ** -0.5, 4.0)
    final_offset_vector = centred(key_list[5], (CZ,), 0.5, 3.0, (), jnp.float32)
    return {"homolog_embedding": homolog_embedding, "standardizer_scaling": standardizer_scaling, "standardizer_shift": standardizer_shift, "paired_projector_matrix": paired_projector_matrix, "final_projector_matrix": final_projector_matrix, "final_offset_vector": final_offset_vector}


def standardize_features(homolog_embedding, standardizer_scaling, standardizer_shift):
    element_number = homolog_embedding.astype(jnp.float32)
    centre = lax.optimization_barrier(jnp.mean(element_number, axis=-1, keepdims=True))
    spread = lax.optimization_barrier(jnp.mean((element_number - centre) ** 2, axis=-1, keepdims=True))
    return ((element_number - centre) * lax.rsqrt(spread + 1e-05) * standardizer_scaling + standardizer_shift).astype(jnp.bfloat16)

def reference(homolog_embedding, standardizer_scaling, standardizer_shift, paired_projector_matrix, final_projector_matrix, final_offset_vector):
    standardized_embedding = standardize_features(homolog_embedding, standardizer_scaling, standardizer_shift)
    unrolled_pairs = standardized_embedding.reshape(HOMOLOG_ROWS * CHAIN_POSITIONS, FEATURE_DEPTH_M)
    projected = jnp.dot(unrolled_pairs, paired_projector_matrix, preferred_element_type=jnp.float32).astype(jnp.bfloat16)
    projected = projected.reshape(HOMOLOG_ROWS, CHAIN_POSITIONS, 2 * CP)
    left = projected[..., :CP].astype(jnp.float32)
    right = projected[..., CP:].astype(jnp.float32)
    block_rows = 8
    starts = jnp.arange(CHAIN_POSITIONS // block_rows, dtype=jnp.int32) * block_rows

    def one_block(start):
        acc = jnp.zeros((block_rows * CHAIN_POSITIONS, CZ), jnp.float32)
        for group in range(N_SEQ):
            left_group = left[group * SEQ_DEV:(group + 1) * SEQ_DEV]
            right_group = right[group * SEQ_DEV:(group + 1) * SEQ_DEV]
            left_rows = lax.dynamic_slice_in_dim(left_group, start, block_rows, 1)
            outer = jnp.einsum('sic,sjd->ijcd', left_rows, right_group) / HOMOLOG_ROWS
            outer = outer.astype(jnp.bfloat16).reshape(block_rows * CHAIN_POSITIONS, CP * CP)
            acc = acc + jnp.dot(outer, final_projector_matrix, preferred_element_type=jnp.float32)
        return (acc + final_offset_vector).astype(jnp.bfloat16).reshape(block_rows, CHAIN_POSITIONS, CZ)
    blocks = lax.map(one_block, starts)
    return blocks.reshape(CHAIN_POSITIONS, CHAIN_POSITIONS, CZ)
```

```python
import jax
import jax.numpy as jnp
from jax import lax
from jax.experimental import pallas as pl
from jax.experimental.pallas import tpu as pltpu
from jax.sharding import PartitionSpec as P

F32 = jnp.float32
BF16 = jnp.bfloat16
MESH = pl.DeviceIdType.MESH
NT = (((1,), (1,)), ((), ()))


def remote(src, dst, send_sem, recv_sem, dev):
    return pltpu.make_async_remote_copy(
        src_ref=src, dst_ref=dst, send_sem=send_sem, recv_sem=recv_sem, device_id=dev, device_id_type=MESH
    )


def standardize(x, gain, shift):
    centre = jnp.mean(x, axis=-1, keepdims=True)
    away = x - centre
    spread = jnp.mean(away * away, axis=-1, keepdims=True)
    return (away * lax.rsqrt(spread + 1e-05) * gain + shift).astype(BF16)


def project(x_ref, gain, shift, w64, lsend, rsend):
    pieces = []
    for k in range(4):
        normed = standardize(x_ref[k].astype(F32), gain[...], shift[...])
        both = lax.dot_general(w64[...], normed, NT, preferred_element_type=F32)
        lsend[k * 32:(k + 1) * 32, :] = both[:32].astype(BF16)
        pieces.append(both[32:])
    for dc in range(4):
        rows = jnp.concatenate([p[dc * 8:(dc + 1) * 8] for p in pieces], axis=0).astype(BF16)
        for sl in range(2):
            rsend[sl, dc] = rows[:, sl * 128:(sl + 1) * 128]


def arrange_final(wfin, wide, w2t):
    wide[...] = wfin[...].astype(F32)
    for d2 in range(2):
        rows = jnp.concatenate([wide[pl.ds(dp * 2 + d2, 32, stride=32), :] for dp in range(16)], axis=0)
        w2t[d2 * 128:(d2 + 1) * 128, :] = rows.T.astype(BF16)


def pair_rows(ib, lt, rt, w2t, outer, off, out, scale):
    rows = pl.ds(pl.multiple_of(ib * 256, 256), 256)
    left = jnp.concatenate([lt[0, rows, :], lt[1, rows, :]], axis=1)
    for dc in range(4):
        right = jnp.concatenate([rt[s, dc * 512:(dc + 1) * 512, :] for s in range(4)], axis=1)
        p = lax.dot_general(left, right, NT, preferred_element_type=F32).astype(BF16)
        for i in range(8):
            for dp in range(4):
                outer[(dc * 4 + dp) * 32:(dc * 4 + dp + 1) * 32, i * 128:(i + 1) * 128] = p[
                    i * 32:(i + 1) * 32, dp * 128:(dp + 1) * 128
                ]
    res = jnp.dot(w2t[...], outer[...], preferred_element_type=F32)
    first = lax.broadcasted_iota(jnp.int32, (128, 128), 1) < 64
    for i in range(8):
        both = jnp.where(first, res[:128, i * 128:(i + 1) * 128], res[128:, i * 128:(i + 1) * 128]).T
        out[ib * 8 + i] = ((both[:64] + both[64:]) * scale + off[...]).astype(BF16)


def kernel(x_ref, gain, shift, w64, wfin, off, out,
           lt, rt, lsend, rsend, stage, stage_f, wide, w2t, outer,
           z_send, z_recv, x_send, x_recv, s_send, s_recv, a_send, a_recv, b_send, b_recv, p_send, p_recv):
    q, ri, rj = lax.axis_index("seq"), lax.axis_index("ri"), lax.axis_index("rj")
    y, c, zl, xx = ri // 2, ri % 2, rj // 4, rj % 4
    half = zl // 2
    way = 1 - 2 * c
    self_z = half == q
    self_s = jnp.logical_and(rj == ri, (ri % 4) // 2 == q)

    def at_x(n):
        return (q, ri, zl * 4 + (xx + n + 4) % 4)

    def at_y(n):
        return (q, 2 * ((y + n + 8) % 8) + c, rj)

    peer = (q, 2 * y + 1 - c, rj)

    barrier = pltpu.get_barrier_semaphore()

    def greet(dev):
        pl.semaphore_signal(barrier, inc=1, device_id=dev, device_id_type=MESH)

    for a in range(2):
        for b in range(2):
            me = jnp.logical_and(a == q, 2 * q + b == zl)

            @pl.when(jnp.logical_not(me))
            def _():
                greet((a, ri, 4 * (2 * q + b) + xx))

    for n in (1, -1):
        greet(at_x(n))
        greet(at_y(n))
    greet(peer)

    def greet_source(s, carry):
        me = jnp.logical_and(self_s, s == rj)

        @pl.when(jnp.logical_not(me))
        def _():
            greet(((ri % 4) // 2, rj, s))

        return carry

    lax.fori_loop(0, 16, greet_source, 0)

    project(x_ref, gain, shift, w64, lsend, rsend)

    pl.semaphore_wait(barrier, 25 - self_z.astype(jnp.int32) - self_s.astype(jnp.int32))

    def scatter(n, dc, sl, qd):
        dev = (qd, 4 * dc + 2 * q + sl, ri)
        me = jnp.logical_and(jnp.logical_and(qd == q, rj == ri), 4 * dc + 2 * q + sl == ri)
        dst = stage.at[pl.ds(pl.multiple_of(rj * 32, 32), 32), :]
        return me, remote(rsend.at[sl, dc], dst, s_send.at[n], s_recv.at[rj], dev), pltpu.make_async_copy(
            rsend.at[sl, dc], dst, s_recv.at[rj]
        )

    combos = [(dc, sl, qd) for dc in range(4) for sl in range(2) for qd in range(2)]
    for n, combo in enumerate(combos):
        me, far, near = scatter(n, *combo)

        @pl.when(me)
        def _():
            near.start()

        @pl.when(jnp.logical_not(me))
        def _():
            far.start()

    z_slot = lt.at[q, pl.ds(pl.multiple_of(((zl % 2) * 4 + xx) * 128, 128), 128), :]
    z_sem = z_recv.at[q * 2 + zl % 2]

    def z_copy(t):
        return remote(lsend, z_slot, z_send.at[t], z_sem, (half, ri, 4 * ((zl + t) % 4) + xx))

    for t in (3, 2, 1):
        z_copy(t).start()

    @pl.when(self_z)
    def _():
        pltpu.make_async_copy(lsend, z_slot, z_sem).start()

    @pl.when(jnp.logical_not(self_z))
    def _():
        z_copy(0).start()

    arrange_final(wfin, wide, w2t)

    def slot(m):
        return rt.at[m % 4, pl.ds(pl.multiple_of((m // 4) * 512, 512), 512), :]

    for s in range(16):
        piece = stage.at[s * 32:(s + 1) * 32, :]
        pltpu.make_async_copy(piece, piece, s_recv.at[s]).wait()
    stage_f[...] = stage[...].astype(F32)
    for d in range(8):
        rt[ri % 4, pl.ds(pl.multiple_of((ri // 4) * 512 + d * 64, 64), 64), :] = stage_f[
            pl.ds(d, 64, stride=8), :
        ].astype(BF16)

    def ring_a(k):
        s = slot(2 * ((y - way * k + 8) % 8) + c)
        return remote(s, s, a_send.at[k], a_recv.at[k], at_y(way))

    def ring_b(k):
        s = slot(2 * ((y + way * k + 8) % 8) + c)
        return remote(s, s, b_send.at[k], b_recv.at[k], at_y(-way))

    def here(n, step):
        s = slot(2 * ((y + step + 8) % 8) + c)
        return remote(s, s, p_send.at[n], p_recv.at[n], peer)

    def land(sem, m):
        s = slot(m)
        pltpu.make_async_copy(s, s, sem).wait()

    ring_a(0).start()
    ring_b(0).start()
    here(0, 0).start()

    def x_slot(a, b, n):
        return lt.at[a, pl.ds(pl.multiple_of((b * 4 + (xx + n + 4) % 4) * 128, 128), 128), :]

    def x_copy(a, b, n, ahead):
        g = (a * 2 + b) * 3
        if n == 0:
            return remote(x_slot(a, b, 0), x_slot(a, b, 0), x_send.at[g + ahead], x_recv.at[g + ahead],
                          at_x(way if ahead == 0 else -way))
        return remote(x_slot(a, b, -way), x_slot(a, b, -way), x_send.at[g + 2], x_recv.at[g + 2], at_x(way))

    def x_land(a, b, kind):
        s = x_slot(a, b, (-way, way, 2)[kind])
        pltpu.make_async_copy(s, s, x_recv.at[(a * 2 + b) * 3 + kind]).wait()

    pieces = [(a, b) for a in range(2) for b in range(2)]

    for a, b in pieces:
        s = x_slot(a, b, 0)
        pltpu.make_async_copy(s, s, z_recv.at[a * 2 + b]).wait()
        x_copy(a, b, 0, 0).start()
        x_copy(a, b, 0, 1).start()

    def ring_step(k):
        land(a_recv.at[k - 1], 2 * ((y - way * k + 8) % 8) + c)
        if k < 4:
            ring_a(k).start()
        here(k, -way * k).start()
        if k < 4:
            land(b_recv.at[k - 1], 2 * ((y + way * k + 8) % 8) + c)
            if k < 3:
                ring_b(k).start()
            here(4 + k, way * k).start()

    ring_step(1)
    for a, b in pieces:
        x_land(a, b, 0)
        x_copy(a, b, 1, 0).start()
    ring_step(2)
    ring_step(3)
    for a, b in pieces:
        x_land(a, b, 1)
        x_land(a, b, 2)
    ring_step(4)
    land(p_recv.at[0], 2 * y + 1 - c)
    for k in range(1, 5):
        land(p_recv.at[k], 2 * ((y + way * k + 8) % 8) + 1 - c)
    for k in range(1, 4):
        land(p_recv.at[4 + k], 2 * ((y - way * k + 8) % 8) + 1 - c)

    scale = 1.0 / (2 * x_ref.shape[1])

    def block(ib, carry):
        pair_rows(ib, lt, rt, w2t, outer, off, out, scale)
        return carry

    lax.fori_loop(0, 4, block, 0)

    for n, combo in enumerate(combos):
        me, far, near = scatter(n, *combo)

        @pl.when(jnp.logical_not(me))
        def _():
            far.wait_send()

    for t in (1, 2, 3):
        z_copy(t).wait_send()

    @pl.when(jnp.logical_not(self_z))
    def _():
        z_copy(0).wait_send()

    for k in range(4):
        ring_a(k).wait_send()
    for k in range(3):
        ring_b(k).wait_send()
    here(0, 0).wait_send()
    for k in range(1, 5):
        here(k, -way * k).wait_send()
    for k in range(1, 4):
        here(4 + k, way * k).wait_send()
    for a, b in pieces:
        x_copy(a, b, 0, 0).wait_send()
        x_copy(a, b, 0, 1).wait_send()
        x_copy(a, b, 1, 0).wait_send()


def per_device(embedding, gain, shift, projector, final, offset):
    dma = pltpu.SemaphoreType.DMA
    vmem = pl.BlockSpec(memory_space=pltpu.VMEM)
    return pl.pallas_call(
        kernel,
        out_shape=jax.ShapeDtypeStruct((32, 64, 128), BF16),
        in_specs=[vmem] * 6,
        out_specs=vmem,
        scratch_shapes=[
            pltpu.VMEM((2, 1024, 256), BF16),
            pltpu.VMEM((4, 2048, 128), BF16),
            pltpu.VMEM((128, 256), BF16),
            pltpu.VMEM((2, 4, 32, 128), BF16),
            pltpu.VMEM((512, 128), BF16),
            pltpu.VMEM((512, 128), F32),
            pltpu.VMEM((1024, 128), F32),
            pltpu.VMEM((256, 512), BF16),
            pltpu.VMEM((512, 1024), BF16),
            dma((4,)), dma((4,)), dma((12,)), dma((12,)), dma((16,)), dma((16,)),
            dma((4,)), dma((4,)), dma((3,)), dma((3,)), dma((8,)), dma((8,)),
        ],
        compiler_params=pltpu.CompilerParams(
            collective_id=0, has_side_effects=True, vmem_limit_bytes=48 << 20
        ),
    )(jnp.swapaxes(embedding, 0, 1), gain.reshape(1, -1), shift.reshape(1, -1), projector.T, final, offset.reshape(1, -1))


def solution(mesh):
    in_specs = (P("seq", ("ri", "rj"), None), P(), P(), P(), P(), P())
    return jax.shard_map(
        per_device, mesh=mesh, in_specs=in_specs, out_specs=P(("ri", "seq"), "rj", None), check_vma=False
    )
```

```python
import jax
import jax.numpy as jnp
from jax import lax
from jax.experimental import pallas as pl
from jax.experimental.pallas import tpu as pltpu
from jax.sharding import PartitionSpec as P

F32 = jnp.float32
BF16 = jnp.bfloat16
MESH = pl.DeviceIdType.MESH
NT = (((1,), (1,)), ((), ()))


def remote(src, dst, send_sem, recv_sem, dev):
    return pltpu.make_async_remote_copy(
        src_ref=src, dst_ref=dst, send_sem=send_sem, recv_sem=recv_sem, device_id=dev, device_id_type=MESH
    )


def standardize(x, gain, shift):
    centre = jnp.mean(x, axis=-1, keepdims=True)
    away = x - centre
    spread = jnp.mean(away * away, axis=-1, keepdims=True)
    return (away * lax.rsqrt(spread + 1e-05) * gain + shift).astype(BF16)


def project(x_ref, gain, shift, w64, lsend, rsend):
    pieces = []
    for k in range(4):
        normed = standardize(x_ref[k].astype(F32), gain[...], shift[...])
        both = lax.dot_general(w64[...], normed, NT, preferred_element_type=F32)
        lsend[k * 32:(k + 1) * 32, :] = both[:32].astype(BF16)
        pieces.append(both[32:])
    for dc in range(4):
        rows = jnp.concatenate([p[dc * 8:(dc + 1) * 8] for p in pieces], axis=0).astype(BF16)
        for sl in range(2):
            rsend[sl, dc] = rows[:, sl * 128:(sl + 1) * 128]


def arrange_final(wfin, wide, w2t):
    wide[...] = wfin[...].astype(F32)
    for d2 in range(2):
        rows = jnp.concatenate([wide[pl.ds(dp * 2 + d2, 32, stride=32), :] for dp in range(16)], axis=0)
        turned = rows.T.astype(BF16)
        for dc in range(4):
            w2t[dc, d2 * 128:(d2 + 1) * 128, :] = turned[:, dc * 128:(dc + 1) * 128]


def outer_product(ib, pos, dc, lt, rt, outer):
    rows = pl.ds(pl.multiple_of(ib * 256, 256), 256)
    left = jnp.concatenate([lt[0, rows, :], lt[1, rows, :]], axis=1)
    right = jnp.concatenate([rt[sc, pl.ds(dc * 8, 8)].reshape(512, 128) for sc in range(4)], axis=1)
    p = lax.dot_general(left, right, NT, preferred_element_type=F32).astype(BF16)
    for i in range(8):
        for dp in range(4):
            outer[ib, (pos * 4 + dp) * 32:(pos * 4 + dp + 1) * 32, i * 128:(i + 1) * 128] = p[
                i * 32:(i + 1) * 32, dp * 128:(dp + 1) * 128
            ]


def last_product(ib, t, dcs, w2t, outer):
    weights = jnp.concatenate([w2t[dc] for dc in dcs], axis=1)
    res = jnp.dot(weights, outer[ib, t * 256:(t + 1) * 256, :], preferred_element_type=F32)
    lane = lax.broadcasted_iota(jnp.int32, (128, 1024), 1)
    return jnp.where(lane % 128 < 64, res[:128], res[128:])


def kernel(x_ref, gain, shift, w64, wfin, off, out,
           lt, rt, lsend, rsend, stage, stage_f, wide, w2t, outer, partial,
           z_send, z_recv, f_send, x_send, x_recv, s_send, s_recv, a_send, a_recv, b_send, b_recv, p_send, p_recv):
    q, ri, rj = lax.axis_index("seq"), lax.axis_index("ri"), lax.axis_index("rj")
    y, c, zl, xx = ri // 2, ri % 2, rj // 4, rj % 4
    half = zl // 2
    way = 1 - 2 * c
    self_z = half == q
    self_s = rj == ri

    def at_x(n):
        return (q, ri, zl * 4 + (xx + n + 4) % 4)

    def at_y(n):
        return (q, 2 * ((y + n + 8) % 8) + c, rj)

    def at_w(h, w):
        return (h, ri, (w + h * (3 - 2 * w)) * 4 + xx)

    peer = (q, 2 * y + 1 - c, rj)
    place = zl + q * (3 - 2 * zl)
    src = 4 * (q + half - 2 * q * half) + (zl % 2 + half - 2 * (zl % 2) * half)

    barrier = pltpu.get_barrier_semaphore()

    def greet(dev):
        pl.semaphore_signal(barrier, inc=1, device_id=dev, device_id_type=MESH)

    def greet_source(s, carry):
        for a in range(2):
            me = jnp.logical_and(self_s, jnp.logical_and(a == q, s == rj))

            @pl.when(jnp.logical_not(me))
            def _():
                greet((a, rj, s))

        return carry

    lax.fori_loop(0, 16, greet_source, 0)

    def greet_place(w):
        @pl.when(w >= 0)
        def _():
            greet((jnp.where(w >= 4, 1 - q, q), ri, jnp.where(q == 0, w % 4, 3 - w % 4) * 4 + xx))

    def table(*values):
        v = values[3]
        for n in (2, 1, 0):
            v = jnp.where(place == n, values[n], v)
        return v

    greet_place(table(1, 0, 0, 1))
    greet_place(table(5, 4, 1, 4))
    greet_place(table(1, 0, 5, 2))
    greet_place(table(-1, -1, 3, 2))
    for n in (1, -1):
        greet(at_x(n))
        greet(at_y(n))
    greet(peer)

    project(x_ref, gain, shift, w64, lsend, rsend)

    z_targets = jnp.where(src == 1, 3, 2) + jnp.where(place == 2, 2, 1)
    pl.semaphore_wait(barrier, 32 - self_s.astype(jnp.int32) + z_targets + 5)

    def scatter(n, dc, sl, qd, yh):
        dev = (qd, 2 * (dc + 4 * yh) + sl, ri)
        me = jnp.logical_and(jnp.logical_and(qd == q, rj == ri), 2 * (dc + 4 * yh) + sl == ri)
        dst = stage.at[q, pl.ds(pl.multiple_of(rj * 32, 32), 32), :]
        sem = s_recv.at[q * 16 + rj]
        return me, remote(rsend.at[sl, dc], dst, s_send.at[n], sem, dev), pltpu.make_async_copy(
            rsend.at[sl, dc], dst, sem
        )

    combos = [(dc, sl, qd, yh) for dc in range(4) for sl in range(2) for qd in range(2) for yh in range(2)]
    for n, combo in enumerate(combos):
        me, far, near = scatter(n, *combo)

        @pl.when(me)
        def _():
            near.start()

        @pl.when(jnp.logical_not(me))
        def _():
            far.start()

    def left_slot(h, e, x):
        a = e // 2 + h - 2 * (e // 2) * h
        b = e % 2 + h - 2 * (e % 2) * h
        return lt.at[a, pl.ds(pl.multiple_of((b * 4 + x) * 128, 128), 128), :]

    own = src % 4 + 2 * (src // 4)
    z_slot = left_slot(half, own, xx)

    def z_copy(t):
        w = (1 - src % 2, jnp.where(src == 4, 3, 2), 3)[t]
        return remote(lsend, z_slot, z_send.at[t], z_recv.at[own], at_w(half, w))

    z_copy(1).start()

    @pl.when(src == 1)
    def _():
        z_copy(2).start()

    z_copy(0).start()

    @pl.when(self_z)
    def _():
        pltpu.make_async_copy(lsend, z_slot, z_recv.at[own]).start()

    arrange_final(wfin, wide, w2t)

    order = [table(0, 1, 1, 2), table(1, 0, 0, 1), table(3, 2, 3, 0), table(2, 3, 2, 3)]
    passing = [place == 3, place == 2, place <= 2]

    def onward(p):
        e = order[p]
        s = left_slot(q, e, xx)
        return remote(s, s, f_send.at[p], z_recv.at[e], at_w(q, place + 1 - 2 * (place % 2)))

    def x_copy(p, kind):
        e = order[p]
        s = left_slot(q, e, xx if kind < 2 else (xx - way + 4) % 4)
        return remote(s, s, x_send.at[e * 3 + kind], x_recv.at[e * 3 + kind], at_x(-way if kind == 1 else way))

    def x_land(p, kind):
        e = order[p]
        s = left_slot(q, e, (xx + (-way, way, 2)[kind] + 4) % 4)
        pltpu.make_async_copy(s, s, x_recv.at[e * 3 + kind]).wait()

    def z_land(p):
        e = order[p]
        s = left_slot(q, e, xx)
        pltpu.make_async_copy(s, s, z_recv.at[e]).wait()
        if p < 3:
            @pl.when(passing[p])
            def _():
                onward(p).start()
        x_copy(p, 0).start()
        x_copy(p, 1).start()

    def x_step(p):
        x_land(p, 0)
        x_copy(p, 2).start()

    near_zl = (zl, zl + 1 - 2 * (zl % 2), (zl + 2) % 4, 3 - zl)
    parts = [(q, near_zl[n]) for n in (0, 1, 2, 3)] + [(1 - q, near_zl[n]) for n in (3, 2, 1, 0)]

    def part(step, g):
        a, z = parts[g]
        return rt.at[2 * a + c, pl.ds(((y + step + 8) % 4) * 8, 8), pl.ds(pl.multiple_of(z * 16, 16), 16), :]

    def quarter(step, a, core):
        return rt.at[2 * a + core, pl.ds(((y + step + 8) % 4) * 8, 8)]

    def ring_a(k, g):
        s = part(-way * k, g)
        return remote(s, s, a_send.at[k * 8 + g], a_recv.at[k * 8 + g], at_y(way))

    def ring_b(g):
        s = part(0, g)
        return remote(s, s, b_send.at[g], b_recv.at[g], at_y(-way))

    steps = (0, -1, 1, -2)

    def here(kind, n):
        a = parts[n * 4][0]
        s = quarter(way * steps[kind], a, c)
        return remote(s, s, p_send.at[kind * 2 + a], p_recv.at[kind * 2 + a], peer)

    def here_land(kind):
        for a in range(2):
            s = quarter(-way * steps[kind], a, 1 - c)
            pltpu.make_async_copy(s, s, p_recv.at[kind * 2 + a]).wait()

    def land(sem, s):
        pltpu.make_async_copy(s, s, sem).wait()

    def assemble(g):
        a, z = parts[g]
        for x in range(4):
            piece = stage.at[a, pl.ds(pl.multiple_of((z * 4 + x) * 32, 32), 32), :]
            land(s_recv.at[a * 16 + z * 4 + x], piece)
        stage_f[g] = stage[a, pl.ds(pl.multiple_of(z * 128, 128), 128), :].astype(F32)
        for d in range(8):
            rt[2 * a + c, (y % 4) * 8 + d, pl.ds(pl.multiple_of(z * 16, 16), 16), :] = stage_f[
                g, pl.ds(d, 16, stride=8), :
            ].astype(BF16)
        ring_a(0, g).start()
        ring_b(g).start()
        if g % 4 == 3:
            here(0, g // 4).start()

    def pass_on(g):
        land(a_recv.at[g], part(-way, g))
        ring_a(1, g).start()
        land(b_recv.at[g], part(way, g))
        if g % 4 == 3:
            here(1, g // 4).start()
            here(2, g // 4).start()

    z_land(0)
    z_land(1)
    for g in range(4):
        assemble(g)
    z_land(2)
    for g in range(4, 8):
        assemble(g)
    z_land(3)
    for g in range(8):
        pass_on(g)
        if g % 2 == 1:
            x_step(g // 2)
    for p in range(4):
        x_land(p, 1)
        x_land(p, 2)
    for kind in range(3):
        here_land(kind)

    dcs = [(y + n) % 4 for n in (0, 1, 3, 2)]

    def early(ib, carry):
        for pos in range(3):
            outer_product(ib, pos, dcs[pos], lt, rt, outer)
        partial[ib] = last_product(ib, 0, dcs[:2], w2t, outer)
        return carry

    lax.fori_loop(0, 4, early, 0)

    for g in range(8):
        land(a_recv.at[8 + g], part(-way * 2, g))
        if g % 4 == 3:
            here(3, g // 4).start()
    here_land(3)

    scale = 1.0 / (2 * x_ref.shape[1])

    def late(ib, carry):
        outer_product(ib, 3, dcs[3], lt, rt, outer)
        total = partial[ib] + last_product(ib, 1, dcs[2:], w2t, outer)
        for i in range(8):
            both = total[:, i * 128:(i + 1) * 128].T
            out[ib * 8 + i] = ((both[:64] + both[64:]) * scale + off[...]).astype(BF16)
        return carry

    lax.fori_loop(0, 4, late, 0)

    for n, combo in enumerate(combos):
        me, far, near = scatter(n, *combo)

        @pl.when(jnp.logical_not(me))
        def _():
            far.wait_send()

    z_copy(0).wait_send()
    z_copy(1).wait_send()

    @pl.when(src == 1)
    def _():
        z_copy(2).wait_send()

    for p in range(3):
        @pl.when(passing[p])
        def _():
            onward(p).wait_send()
    for p in range(4):
        for kind in range(3):
            x_copy(p, kind).wait_send()
    for g in range(8):
        ring_a(0, g).wait_send()
        ring_a(1, g).wait_send()
        ring_b(g).wait_send()
    for kind in range(4):
        for n in range(2):
            here(kind, n).wait_send()


def per_device(embedding, gain, shift, projector, final, offset):
    dma = pltpu.SemaphoreType.DMA
    operands = (jnp.swapaxes(embedding, 0, 1), gain.reshape(1, -1), shift.reshape(1, -1), projector.T, final, offset.reshape(1, -1))
    return pl.pallas_call(
        kernel,
        out_shape=jax.ShapeDtypeStruct((32, 64, 128), BF16),
        in_specs=[pl.BlockSpec(memory_space=pltpu.VMEM)] * 6,
        out_specs=pl.BlockSpec(memory_space=pltpu.VMEM),
        scratch_shapes=[
            pltpu.VMEM((2, 1024, 256), BF16),
            pltpu.VMEM((4, 32, 64, 128), BF16),
            pltpu.VMEM((128, 256), BF16),
            pltpu.VMEM((2, 4, 32, 128), BF16),
            pltpu.VMEM((2, 512, 128), BF16),
            pltpu.VMEM((8, 128, 128), F32),
            pltpu.VMEM((1024, 128), F32),
            pltpu.VMEM((4, 256, 128), BF16),
            pltpu.VMEM((4, 512, 1024), BF16),
            pltpu.VMEM((4, 128, 1024), F32),
            dma((3,)), dma((4,)), dma((3,)), dma((12,)), dma((12,)), dma((32,)), dma((32,)),
            dma((16,)), dma((16,)), dma((8,)), dma((8,)), dma((8,)), dma((8,)),
        ],
        compiler_params=pltpu.CompilerParams(
            collective_id=0, has_side_effects=True, vmem_limit_bytes=48 << 20
        ),
    )(*operands)


def solution(mesh):
    in_specs = (P("seq", ("ri", "rj"), None), P(), P(), P(), P(), P())
    return jax.shard_map(
        per_device, mesh=mesh, in_specs=in_specs, out_specs=P(("ri", "seq"), "rj", None), check_vma=False
    )
```

```python
import jax
import jax.numpy as jnp
from jax import lax
from jax.experimental import pallas as pl
from jax.experimental.pallas import tpu as pltpu
from jax.sharding import PartitionSpec as P

F32 = jnp.float32
BF16 = jnp.bfloat16
MESH = pl.DeviceIdType.MESH
NT = (((1,), (1,)), ((), ()))


def remote(src, dst, send_sem, recv_sem, dev):
    return pltpu.make_async_remote_copy(
        src_ref=src, dst_ref=dst, send_sem=send_sem, recv_sem=recv_sem, device_id=dev, device_id_type=MESH
    )


def standardize(x, gain, shift):
    centre = jnp.mean(x, axis=-1, keepdims=True)
    away = x - centre
    spread = jnp.mean(away * away, axis=-1, keepdims=True)
    return (away * lax.rsqrt(spread + 1e-05) * gain + shift).astype(BF16)


def project(x_ref, gain, shift, w64, lsend, rsend):
    pieces = []
    for k in range(4):
        normed = standardize(x_ref[k].astype(F32), gain[...], shift[...])
        both = lax.dot_general(w64[...], normed, NT, preferred_element_type=F32)
        lsend[k * 32:(k + 1) * 32, :] = both[:32].astype(BF16)
        pieces.append(both[32:])
    for dc in range(4):
        rows = jnp.concatenate([p[dc * 8:(dc + 1) * 8] for p in pieces], axis=0).astype(BF16)
        for sl in range(2):
            rsend[dc, sl] = rows[:, sl * 128:(sl + 1) * 128]


def arrange_final(wfin, wide, w2t):
    wide[...] = wfin[...].astype(F32)
    for d2 in range(2):
        rows = jnp.concatenate([wide[pl.ds(dp * 2 + d2, 32, stride=32), :] for dp in range(16)], axis=0)
        turned = rows.T.astype(BF16)
        for dc in range(4):
            w2t[dc, d2 * 128:(d2 + 1) * 128, :] = turned[:, dc * 128:(dc + 1) * 128]


def outer_product(ib, pos, dc, lt, rt, outer):
    rows = pl.ds(pl.multiple_of(ib * 256, 256), 256)
    left = jnp.concatenate([lt[0, rows, :], lt[1, rows, :]], axis=1)
    right = jnp.concatenate([rt[sc, pl.ds(dc * 8, 8)].reshape(512, 128) for sc in range(4)], axis=1)
    p = lax.dot_general(left, right, NT, preferred_element_type=F32).astype(BF16)
    for i in range(8):
        for dp in range(4):
            outer[ib, (pos * 4 + dp) * 32:(pos * 4 + dp + 1) * 32, i * 128:(i + 1) * 128] = p[
                i * 32:(i + 1) * 32, dp * 128:(dp + 1) * 128
            ]


def last_product(ib, t, dcs, w2t, outer):
    weights = jnp.concatenate([w2t[dc] for dc in dcs], axis=1)
    res = jnp.dot(weights, outer[ib, t * 256:(t + 1) * 256, :], preferred_element_type=F32)
    lane = lax.broadcasted_iota(jnp.int32, (128, 1024), 1)
    return jnp.where(lane % 128 < 64, res[:128], res[128:])


def kernel(x_ref, gain, shift, w64, wfin, off, out,
           lt, rt, lsend, rsend, mid, stage, stage_f, wide, w2t, outer, partial,
           z_send, z_recv, f_send, x_send, x_recv, m_send, m_recv, s_send, s_recv, a_send, a_recv, b_send, b_recv, p_send, p_recv):
    q, ri, rj = lax.axis_index("seq"), lax.axis_index("ri"), lax.axis_index("rj")
    y, c, zl, xx = ri // 2, ri % 2, rj // 4, rj % 4
    half = zl // 2
    way = 1 - 2 * c
    self_z = half == q
    self_s = c == rj % 2
    self_s_count = jnp.where(self_s, 1, 0)

    def at_x(n):
        return (q, ri, zl * 4 + (xx + n + 4) % 4)

    def at_y(n):
        return (q, 2 * ((y + n + 8) % 8) + c, rj)

    def at_w(h, w):
        return (h, ri, (w + h * (3 - 2 * w)) * 4 + xx)

    peer = (q, 2 * y + 1 - c, rj)
    place = zl + q * (3 - 2 * zl)
    src = 4 * (q + half - 2 * q * half) + (zl % 2 + half - 2 * (zl % 2) * half)

    barrier = pltpu.get_barrier_semaphore()

    def greet(dev):
        pl.semaphore_signal(barrier, inc=1, device_id=dev, device_id_type=MESH)

    def greet_source(s, carry):
        for a in range(2):
            me = jnp.logical_and(self_s, jnp.logical_and(a == q, s == rj))

            @pl.when(jnp.logical_not(me))
            def _():
                greet((a, 2 * y + rj % 2, s))

        return carry

    for n in (4, 3, -3, 2, -2, 1, -1):
        greet(at_y(n))
    lax.fori_loop(0, 16, greet_source, 0)

    def greet_place(w):
        @pl.when(w >= 0)
        def _():
            greet((jnp.where(w >= 4, 1 - q, q), ri, jnp.where(q == 0, w % 4, 3 - w % 4) * 4 + xx))

    def table(*values):
        v = values[3]
        for n in (2, 1, 0):
            v = jnp.where(place == n, values[n], v)
        return v

    greet_place(table(1, 0, 0, 1))
    greet_place(table(5, 4, 1, 4))
    greet_place(table(1, 0, 5, 2))
    greet_place(table(-1, -1, 3, 2))
    for n in (1, -1):
        greet(at_x(n))
    greet(peer)

    project(x_ref, gain, shift, w64, lsend, rsend)

    z_targets = jnp.where(src == 1, 3, 2) + jnp.where(place == 2, 2, 1)
    pl.semaphore_wait(barrier, 32 - self_s_count + 7 + z_targets + 3)

    mid_slot = mid.at[y]

    def along_y(n):
        to = (y + n + 8) % 8
        return remote(rsend.at[to % 4], mid_slot, m_send.at[n % 8], m_recv.at[y], at_y(n))

    for n in (4, 3, -3, 2, -2, 1, -1):
        along_y(n).start()
    own_mid = pltpu.make_async_copy(rsend.at[y % 4], mid_slot, m_recv.at[y])
    own_mid.start()

    def left_slot(h, e, x):
        a = e // 2 + h - 2 * (e // 2) * h
        b = e % 2 + h - 2 * (e % 2) * h
        return lt.at[a, pl.ds(pl.multiple_of((b * 4 + x) * 128, 128), 128), :]

    own = src % 4 + 2 * (src // 4)
    z_slot = left_slot(half, own, xx)

    def z_copy(t):
        w = (1 - src % 2, jnp.where(src == 4, 3, 2), 3)[t]
        return remote(lsend, z_slot, z_send.at[t], z_recv.at[own], at_w(half, w))

    z_copy(1).start()

    @pl.when(src == 1)
    def _():
        z_copy(2).start()

    z_copy(0).start()

    @pl.when(self_z)
    def _():
        pltpu.make_async_copy(lsend, z_slot, z_recv.at[own]).start()

    def in_plane(n, sl, qd):
        ys = (y + n + 8) % 8
        dev = (qd, 2 * y + sl, 2 * ys + c)
        me = jnp.logical_and(jnp.logical_and(qd == q, sl == c), 2 * ys + c == rj)
        dst = stage.at[q, pl.ds(pl.multiple_of(rj * 32, 32), 32), :]
        sem = s_recv.at[q * 16 + rj]
        at = (n % 8) * 4 + sl * 2 + qd
        return me, remote(mid.at[ys, sl], dst, s_send.at[at], sem, dev), pltpu.make_async_copy(mid.at[ys, sl], dst, sem)

    hops = (0, 1, -1, 2, -2, 3, -3, 4)

    def spread(n):
        ys = (y + n + 8) % 8
        pltpu.make_async_copy(mid.at[ys], mid.at[ys], m_recv.at[ys]).wait()
        for sl in range(2):
            for qd in range(2):
                me, far, near = in_plane(n, sl, qd)

                @pl.when(me)
                def _():
                    near.start()

                @pl.when(jnp.logical_not(me))
                def _():
                    far.start()

    arrange_final(wfin, wide, w2t)

    order = [table(0, 1, 1, 2), table(1, 0, 0, 1), table(3, 2, 3, 0), table(2, 3, 2, 3)]
    passing = [place == 3, place == 2, place <= 2]

    def onward(p):
        e = order[p]
        s = left_slot(q, e, xx)
        return remote(s, s, f_send.at[p], z_recv.at[e], at_w(q, place + 1 - 2 * (place % 2)))

    def x_copy(p, kind):
        e = order[p]
        s = left_slot(q, e, xx if kind < 2 else (xx - way + 4) % 4)
        return remote(s, s, x_send.at[e * 3 + kind], x_recv.at[e * 3 + kind], at_x(-way if kind == 1 else way))

    def x_land(p, kind):
        e = order[p]
        s = left_slot(q, e, (xx + (-way, way, 2)[kind] + 4) % 4)
        pltpu.make_async_copy(s, s, x_recv.at[e * 3 + kind]).wait()

    def z_land(p):
        e = order[p]
        s = left_slot(q, e, xx)
        pltpu.make_async_copy(s, s, z_recv.at[e]).wait()
        if p < 3:
            @pl.when(passing[p])
            def _():
                onward(p).start()
        x_copy(p, 0).start()
        x_copy(p, 1).start()

    def x_step(p):
        x_land(p, 0)
        x_copy(p, 2).start()

    near_zl = (zl, zl + 1 - 2 * (zl % 2), (zl + 2) % 4, 3 - zl)
    parts = [(q, near_zl[n]) for n in (0, 1, 2, 3)] + [(1 - q, near_zl[n]) for n in (3, 2, 1, 0)]

    def part(step, g):
        a, z = parts[g]
        return rt.at[2 * a + c, pl.ds(((y + step + 8) % 4) * 8, 8), pl.ds(pl.multiple_of(z * 16, 16), 16), :]

    def quarter(step, a, core):
        return rt.at[2 * a + core, pl.ds(((y + step + 8) % 4) * 8, 8)]

    def ring_a(k, g):
        s = part(-way * k, g)
        return remote(s, s, a_send.at[k * 8 + g], a_recv.at[k * 8 + g], at_y(way))

    def ring_b(g):
        s = part(0, g)
        return remote(s, s, b_send.at[g], b_recv.at[g], at_y(-way))

    steps = (0, -1, 1, -2)

    def here(kind, n):
        a = parts[n * 4][0]
        s = quarter(way * steps[kind], a, c)
        return remote(s, s, p_send.at[kind * 2 + a], p_recv.at[kind * 2 + a], peer)

    def here_land(kind):
        for a in range(2):
            s = quarter(-way * steps[kind], a, 1 - c)
            pltpu.make_async_copy(s, s, p_recv.at[kind * 2 + a]).wait()

    def land(sem, s):
        pltpu.make_async_copy(s, s, sem).wait()

    def assemble(g):
        a, z = parts[g]
        for x in range(4):
            piece = stage.at[a, pl.ds(pl.multiple_of((z * 4 + x) * 32, 32), 32), :]
            land(s_recv.at[a * 16 + z * 4 + x], piece)
        stage_f[g] = stage[a, pl.ds(pl.multiple_of(z * 128, 128), 128), :].astype(F32)
        for d in range(8):
            rt[2 * a + c, (y % 4) * 8 + d, pl.ds(pl.multiple_of(z * 16, 16), 16), :] = stage_f[
                g, pl.ds(d, 16, stride=8), :
            ].astype(BF16)
        ring_a(0, g).start()
        ring_b(g).start()
        if g % 4 == 3:
            here(0, g // 4).start()

    def pass_on(g):
        land(a_recv.at[g], part(-way, g))
        ring_a(1, g).start()
        land(b_recv.at[g], part(way, g))
        if g % 4 == 3:
            here(1, g // 4).start()
            here(2, g // 4).start()

    spread(0)
    spread(1)
    spread(-1)
    z_land(0)
    spread(2)
    spread(-2)
    z_land(1)
    spread(3)
    spread(-3)
    spread(4)
    z_land(2)
    x_step(0)
    for g in range(4):
        assemble(g)
    x_step(1)
    z_land(3)
    for g in range(4, 8):
        assemble(g)
    x_step(2)
    for g in range(4):
        pass_on(g)
    x_step(3)
    for g in range(4, 8):
        pass_on(g)
    for p in range(4):
        x_land(p, 1)
        x_land(p, 2)
    for kind in range(3):
        here_land(kind)

    dcs = [(y + n) % 4 for n in (0, 1, 3, 2)]

    for pos in range(3):
        for ib in range(4):
            outer_product(ib, pos, dcs[pos], lt, rt, outer)
    for ib in range(4):
        partial[ib] = last_product(ib, 0, dcs[:2], w2t, outer)

    for g in range(8):
        land(a_recv.at[8 + g], part(-way * 2, g))
        if g % 4 == 3:
            here(3, g // 4).start()
    here_land(3)

    scale = 1.0 / (2 * x_ref.shape[1])

    for ib in range(4):
        outer_product(ib, 3, dcs[3], lt, rt, outer)
    for ib in range(4):
        total = partial[ib] + last_product(ib, 1, dcs[2:], w2t, outer)
        for i in range(8):
            both = total[:, i * 128:(i + 1) * 128].T
            out[ib * 8 + i] = ((both[:64] + both[64:]) * scale + off[...]).astype(BF16)

    for n in hops:
        if n:
            along_y(n).wait_send()
        for sl in range(2):
            for qd in range(2):
                me, far, near = in_plane(n, sl, qd)

                @pl.when(jnp.logical_not(me))
                def _():
                    far.wait_send()

    z_copy(0).wait_send()
    z_copy(1).wait_send()

    @pl.when(src == 1)
    def _():
        z_copy(2).wait_send()

    for p in range(3):
        @pl.when(passing[p])
        def _():
            onward(p).wait_send()
    for p in range(4):
        for kind in range(3):
            x_copy(p, kind).wait_send()
    for g in range(8):
        ring_a(0, g).wait_send()
        ring_a(1, g).wait_send()
        ring_b(g).wait_send()
    for kind in range(4):
        for n in range(2):
            here(kind, n).wait_send()


def per_device(embedding, gain, shift, projector, final, offset):
    dma = pltpu.SemaphoreType.DMA
    operands = (jnp.swapaxes(embedding, 0, 1), gain.reshape(1, -1), shift.reshape(1, -1), projector.T, final, offset.reshape(1, -1))
    return pl.pallas_call(
        kernel,
        out_shape=jax.ShapeDtypeStruct((32, 64, 128), BF16),
        in_specs=[pl.BlockSpec(memory_space=pltpu.VMEM)] * 6,
        out_specs=pl.BlockSpec(memory_space=pltpu.VMEM),
        scratch_shapes=[
            pltpu.VMEM((2, 1024, 256), BF16),
            pltpu.VMEM((4, 32, 64, 128), BF16),
            pltpu.VMEM((128, 256), BF16),
            pltpu.VMEM((4, 2, 32, 128), BF16),
            pltpu.VMEM((8, 2, 32, 128), BF16),
            pltpu.VMEM((2, 512, 128), BF16),
            pltpu.VMEM((8, 128, 128), F32),
            pltpu.VMEM((1024, 128), F32),
            pltpu.VMEM((4, 256, 128), BF16),
            pltpu.VMEM((4, 512, 1024), BF16),
            pltpu.VMEM((4, 128, 1024), F32),
            dma((3,)), dma((4,)), dma((3,)), dma((12,)), dma((12,)), dma((8,)), dma((8,)), dma((32,)), dma((32,)),
            dma((16,)), dma((16,)), dma((8,)), dma((8,)), dma((8,)), dma((8,)),
        ],
        compiler_params=pltpu.CompilerParams(
            collective_id=0, has_side_effects=True, vmem_limit_bytes=48 << 20
        ),
    )(*operands)


def solution(mesh):
    in_specs = (P("seq", ("ri", "rj"), None), P(), P(), P(), P(), P())
    return jax.shard_map(
        per_device, mesh=mesh, in_specs=in_specs, out_specs=P(("ri", "seq"), "rj", None), check_vma=False
    )
```

```python
import jax
import jax.numpy as jnp
from jax import lax
from jax.experimental import pallas as pl
from jax.experimental.pallas import tpu as pltpu
from jax.sharding import PartitionSpec as P

F32 = jnp.float32
BF16 = jnp.bfloat16
MESH = pl.DeviceIdType.MESH
NT = (((1,), (1,)), ((), ()))


def remote(src, dst, send_sem, recv_sem, dev):
    return pltpu.make_async_remote_copy(
        src_ref=src, dst_ref=dst, send_sem=send_sem, recv_sem=recv_sem, device_id=dev, device_id_type=MESH
    )


def standardize(x, gain, shift):
    centre = jnp.mean(x, axis=-1, keepdims=True)
    away = x - centre
    spread = jnp.mean(away * away, axis=-1, keepdims=True)
    return (away * lax.rsqrt(spread + 1e-05) * gain + shift).astype(BF16)


def project(x_ref, gain, shift, w64, lsend, rsend):
    pieces = []
    for k in range(4):
        normed = standardize(x_ref[k].astype(F32), gain[...], shift[...])
        both = lax.dot_general(w64[...], normed, NT, preferred_element_type=F32)
        lsend[k * 32:(k + 1) * 32, :] = both[:32].astype(BF16)
        pieces.append(both[32:])
    for dc in range(4):
        rows = jnp.concatenate([p[dc * 8:(dc + 1) * 8] for p in pieces], axis=0).astype(BF16)
        for sl in range(2):
            rsend[dc, sl] = rows[:, sl * 128:(sl + 1) * 128]


def arrange_final(wfin, wide, w2t):
    wide[...] = wfin[...].astype(F32)
    for d2 in range(2):
        rows = jnp.concatenate([wide[pl.ds(dp * 2 + d2, 32, stride=32), :] for dp in range(16)], axis=0)
        turned = rows.T.astype(BF16)
        for dc in range(4):
            w2t[dc, d2 * 128:(d2 + 1) * 128, :] = turned[:, dc * 128:(dc + 1) * 128]


def outer_product(ib, pos, dc, lt, rt, outer):
    rows = pl.ds(pl.multiple_of(ib * 256, 256), 256)
    left = jnp.concatenate([lt[0, rows, :], lt[1, rows, :]], axis=1)
    right = jnp.concatenate([rt[sc, pl.ds(dc * 8, 8)].reshape(512, 128) for sc in range(4)], axis=1)
    p = lax.dot_general(left, right, NT, preferred_element_type=F32).astype(BF16)
    for i in range(8):
        for dp in range(4):
            outer[ib, (pos * 4 + dp) * 32:(pos * 4 + dp + 1) * 32, i * 128:(i + 1) * 128] = p[
                i * 32:(i + 1) * 32, dp * 128:(dp + 1) * 128
            ]


def last_product(ib, t, dcs, w2t, outer):
    weights = jnp.concatenate([w2t[dc] for dc in dcs], axis=1)
    res = jnp.dot(weights, outer[ib, t * 256:(t + 1) * 256, :], preferred_element_type=F32)
    lane = lax.broadcasted_iota(jnp.int32, (128, 1024), 1)
    return jnp.where(lane % 128 < 64, res[:128], res[128:])


def kernel(x_ref, gain, shift, w64, wfin, off, out,
           lt, rt, lsend, rsend, mid, stage, stage_f, wide, w2t, outer, partial,
           z_send, z_recv, f_send, x_send, x_recv, m_send, m_recv, s_send, s_recv, a_send, a_recv, b_send, b_recv, p_send, p_recv):
    q, ri, rj = lax.axis_index("seq"), lax.axis_index("ri"), lax.axis_index("rj")
    y, c, zl, xx = ri // 2, ri % 2, rj // 4, rj % 4
    half = zl // 2
    way = 1 - 2 * c
    self_z = half == q
    self_s = c == rj % 2
    self_s_count = jnp.where(self_s, 1, 0)

    def at_x(n):
        return (q, ri, zl * 4 + (xx + n + 4) % 4)

    def at_y(n):
        return (q, 2 * ((y + n + 8) % 8) + c, rj)

    def at_w(h, w):
        return (h, ri, (w + h * (3 - 2 * w)) * 4 + xx)

    peer = (q, 2 * y + 1 - c, rj)
    place = zl + q * (3 - 2 * zl)
    src = 4 * (q + half - 2 * q * half) + (zl % 2 + half - 2 * (zl % 2) * half)

    barrier = pltpu.get_barrier_semaphore()

    def greet(dev):
        pl.semaphore_signal(barrier, inc=1, device_id=dev, device_id_type=MESH)

    for s in range(16):
        for a in range(2):
            me = jnp.logical_and(self_s, jnp.logical_and(a == q, s == rj))

            @pl.when(jnp.logical_not(me))
            def _():
                greet((a, 2 * y + rj % 2, s))

    for n in (4, 3, -3, 2, -2, 1, -1):
        greet(at_y(n))

    def greet_place(w):
        @pl.when(w >= 0)
        def _():
            greet((jnp.where(w >= 4, 1 - q, q), ri, jnp.where(q == 0, w % 4, 3 - w % 4) * 4 + xx))

    def table(*values):
        v = values[3]
        for n in (2, 1, 0):
            v = jnp.where(place == n, values[n], v)
        return v

    greet_place(table(1, 0, 0, 1))
    greet_place(table(5, 4, 1, 4))
    greet_place(table(1, 0, 5, 2))
    greet_place(table(-1, -1, 3, 2))
    for n in (1, -1):
        greet(at_x(n))
    greet(peer)

    project(x_ref, gain, shift, w64, lsend, rsend)

    z_targets = jnp.where(src == 1, 3, 2) + jnp.where(place == 2, 2, 1)
    pl.semaphore_wait(barrier, 32 - self_s_count + 7 + z_targets + 3)

    mid_slot = mid.at[y]

    def along_y(n):
        to = (y + n + 8) % 8
        return remote(rsend.at[to % 4], mid_slot, m_send.at[n % 8], m_recv.at[y], at_y(n))

    for n in (4, 3, -3, 2, -2, 1, -1):
        along_y(n).start()
    own_mid = pltpu.make_async_copy(rsend.at[y % 4], mid_slot, m_recv.at[y])
    own_mid.start()

    def left_slot(h, e, x):
        a = e // 2 + h - 2 * (e // 2) * h
        b = e % 2 + h - 2 * (e % 2) * h
        return lt.at[a, pl.ds(pl.multiple_of((b * 4 + x) * 128, 128), 128), :]

    own = src % 4 + 2 * (src // 4)
    z_slot = left_slot(half, own, xx)

    def z_copy(t):
        w = (1 - src % 2, jnp.where(src == 4, 3, 2), 3)[t]
        return remote(lsend, z_slot, z_send.at[t], z_recv.at[own], at_w(half, w))

    z_copy(1).start()

    @pl.when(src == 1)
    def _():
        z_copy(2).start()

    z_copy(0).start()

    @pl.when(self_z)
    def _():
        pltpu.make_async_copy(lsend, z_slot, z_recv.at[own]).start()

    def in_plane(n, sl, qd):
        ys = (y + n + 8) % 8
        dev = (qd, 2 * y + sl, 2 * ys + c)
        me = jnp.logical_and(jnp.logical_and(qd == q, sl == c), 2 * ys + c == rj)
        dst = stage.at[q, pl.ds(pl.multiple_of(rj * 32, 32), 32), :]
        sem = s_recv.at[q * 16 + rj]
        at = (n % 8) * 4 + sl * 2 + qd
        return me, remote(mid.at[ys, sl], dst, s_send.at[at], sem, dev), pltpu.make_async_copy(mid.at[ys, sl], dst, sem)

    hops = (0, 1, -1, 2, -2, 3, -3, 4)

    def spread(n):
        ys = (y + n + 8) % 8
        pltpu.make_async_copy(mid.at[ys], mid.at[ys], m_recv.at[ys]).wait()
        for sl in range(2):
            for qd in range(2):
                me, far, near = in_plane(n, sl, qd)

                @pl.when(me)
                def _():
                    near.start()

                @pl.when(jnp.logical_not(me))
                def _():
                    far.start()

    arrange_final(wfin, wide, w2t)

    order = [table(0, 1, 1, 2), table(1, 0, 0, 1), table(3, 2, 3, 0), table(2, 3, 2, 3)]
    passing = [place == 3, place == 2, place <= 2]

    def onward(p):
        e = order[p]
        s = left_slot(q, e, xx)
        return remote(s, s, f_send.at[p], z_recv.at[e], at_w(q, place + 1 - 2 * (place % 2)))

    def x_copy(p, kind):
        e = order[p]
        s = left_slot(q, e, xx if kind < 2 else (xx - way + 4) % 4)
        return remote(s, s, x_send.at[e * 3 + kind], x_recv.at[e * 3 + kind], at_x(-way if kind == 1 else way))

    def x_land(p, kind):
        e = order[p]
        s = left_slot(q, e, (xx + (-way, way, 2)[kind] + 4) % 4)
        pltpu.make_async_copy(s, s, x_recv.at[e * 3 + kind]).wait()

    def z_land(p):
        e = order[p]
        s = left_slot(q, e, xx)
        pltpu.make_async_copy(s, s, z_recv.at[e]).wait()
        if p < 3:
            @pl.when(passing[p])
            def _():
                onward(p).start()
        x_copy(p, 0).start()
        x_copy(p, 1).start()

    def x_step(p):
        x_land(p, 0)
        x_copy(p, 2).start()

    near_zl = (zl, zl + 1 - 2 * (zl % 2), (zl + 2) % 4, 3 - zl)
    parts = [(q, near_zl[n]) for n in (0, 1, 2, 3)] + [(1 - q, near_zl[n]) for n in (3, 2, 1, 0)]

    def part(step, g):
        a, z = parts[g]
        return rt.at[2 * a + c, pl.ds(((y + step + 8) % 4) * 8, 8), pl.ds(pl.multiple_of(z * 16, 16), 16), :]

    def quarter(step, a, core):
        return rt.at[2 * a + core, pl.ds(((y + step + 8) % 4) * 8, 8)]

    def ring_a(k, g):
        s = part(-way * k, g)
        return remote(s, s, a_send.at[k * 8 + g], a_recv.at[k * 8 + g], at_y(way))

    def ring_b(g):
        s = part(0, g)
        return remote(s, s, b_send.at[g], b_recv.at[g], at_y(-way))

    steps = (0, -1, 1, -2)

    def here(kind, n):
        a = parts[n * 4][0]
        s = quarter(way * steps[kind], a, c)
        return remote(s, s, p_send.at[kind * 2 + a], p_recv.at[kind * 2 + a], peer)

    def here_land(kind):
        for a in range(2):
            s = quarter(-way * steps[kind], a, 1 - c)
            pltpu.make_async_copy(s, s, p_recv.at[kind * 2 + a]).wait()

    def land(sem, s):
        pltpu.make_async_copy(s, s, sem).wait()

    def assemble(g):
        a, z = parts[g]
        for x in range(4):
            piece = stage.at[a, pl.ds(pl.multiple_of((z * 4 + x) * 32, 32), 32), :]
            land(s_recv.at[a * 16 + z * 4 + x], piece)
        stage_f[g] = stage[a, pl.ds(pl.multiple_of(z * 128, 128), 128), :].astype(F32)
        for d in range(8):
            rt[2 * a + c, (y % 4) * 8 + d, pl.ds(pl.multiple_of(z * 16, 16), 16), :] = stage_f[
                g, pl.ds(d, 16, stride=8), :
            ].astype(BF16)
        ring_a(0, g).start()
        ring_b(g).start()
        if g % 4 == 3:
            here(0, g // 4).start()

    def pass_on(g):
        land(a_recv.at[g], part(-way, g))
        ring_a(1, g).start()
        land(b_recv.at[g], part(way, g))
        if g % 4 == 3:
            here(1, g // 4).start()
            here(2, g // 4).start()

    spread(0)
    spread(1)
    spread(-1)
    z_land(0)
    spread(2)
    spread(-2)
    z_land(1)
    spread(3)
    spread(-3)
    spread(4)
    z_land(2)
    x_step(0)
    for g in range(4):
        assemble(g)
    x_step(1)
    z_land(3)
    for g in range(4, 8):
        assemble(g)
    x_step(2)
    for g in range(4):
        pass_on(g)
    x_step(3)
    for g in range(4, 8):
        pass_on(g)
    for n in hops:
        if n:
            along_y(n).wait_send()
        for sl in range(2):
            for qd in range(2):
                me, far, near = in_plane(n, sl, qd)

                @pl.when(jnp.logical_not(me))
                def _():
                    far.wait_send()

    z_copy(0).wait_send()
    z_copy(1).wait_send()

    @pl.when(src == 1)
    def _():
        z_copy(2).wait_send()

    for p in range(3):
        @pl.when(passing[p])
        def _():
            onward(p).wait_send()
    for p in range(4):
        x_land(p, 1)
        x_land(p, 2)
    for kind in range(3):
        here_land(kind)

    dcs = [(y + n) % 4 for n in (0, 1, 3, 2)]

    for pos in range(3):
        for ib in range(4):
            outer_product(ib, pos, dcs[pos], lt, rt, outer)
    for ib in range(4):
        partial[ib] = last_product(ib, 0, dcs[:2], w2t, outer)

    for p in range(4):
        for kind in range(3):
            x_copy(p, kind).wait_send()
    for g in range(8):
        ring_a(0, g).wait_send()
        ring_b(g).wait_send()
    for kind in range(3):
        for n in range(2):
            here(kind, n).wait_send()

    for g in range(8):
        land(a_recv.at[8 + g], part(-way * 2, g))
        if g % 4 == 3:
            here(3, g // 4).start()
    here_land(3)

    scale = 1.0 / (2 * x_ref.shape[1])

    for ib in range(4):
        outer_product(ib, 3, dcs[3], lt, rt, outer)
    for ib in range(4):
        total = partial[ib] + last_product(ib, 1, dcs[2:], w2t, outer)
        for i in range(8):
            both = total[:, i * 128:(i + 1) * 128].T
            out[ib * 8 + i] = ((both[:64] + both[64:]) * scale + off[...]).astype(BF16)

    for g in range(8):
        ring_a(1, g).wait_send()
    for n in range(2):
        here(3, n).wait_send()


def per_device(embedding, gain, shift, projector, final, offset):
    dma = pltpu.SemaphoreType.DMA
    operands = (jnp.swapaxes(embedding, 0, 1), gain.reshape(1, -1), shift.reshape(1, -1), projector.T, final, offset.reshape(1, -1))
    return pl.pallas_call(
        kernel,
        out_shape=jax.ShapeDtypeStruct((32, 64, 128), BF16),
        in_specs=[pl.BlockSpec(memory_space=pltpu.VMEM)] * 6,
        out_specs=pl.BlockSpec(memory_space=pltpu.VMEM),
        scratch_shapes=[
            pltpu.VMEM((2, 1024, 256), BF16),
            pltpu.VMEM((4, 32, 64, 128), BF16),
            pltpu.VMEM((128, 256), BF16),
            pltpu.VMEM((4, 2, 32, 128), BF16),
            pltpu.VMEM((8, 2, 32, 128), BF16),
            pltpu.VMEM((2, 512, 128), BF16),
            pltpu.VMEM((8, 128, 128), F32),
            pltpu.VMEM((1024, 128), F32),
            pltpu.VMEM((4, 256, 128), BF16),
            pltpu.VMEM((4, 512, 1024), BF16),
            pltpu.VMEM((4, 128, 1024), F32),
            dma((3,)), dma((4,)), dma((3,)), dma((12,)), dma((12,)), dma((8,)), dma((8,)), dma((32,)), dma((32,)),
            dma((16,)), dma((16,)), dma((8,)), dma((8,)), dma((8,)), dma((8,)),
        ],
        compiler_params=pltpu.CompilerParams(
            collective_id=0, has_side_effects=True, vmem_limit_bytes=48 << 20
        ),
    )(*operands)


def solution(mesh):
    in_specs = (P("seq", ("ri", "rj"), None), P(), P(), P(), P(), P())
    return jax.shard_map(
        per_device, mesh=mesh, in_specs=in_specs, out_specs=P(("ri", "seq"), "rj", None), check_vma=False
    )
```

```python
import jax
import jax.numpy as jnp
from jax import lax
from jax.experimental import pallas as pl
from jax.experimental.pallas import tpu as pltpu
from jax.sharding import PartitionSpec as P

F32 = jnp.float32
BF16 = jnp.bfloat16
MESH = pl.DeviceIdType.MESH
NT = (((1,), (1,)), ((), ()))


def remote(src, dst, send_sem, recv_sem, dev):
    return pltpu.make_async_remote_copy(
        src_ref=src, dst_ref=dst, send_sem=send_sem, recv_sem=recv_sem, device_id=dev, device_id_type=MESH
    )


def standardize(x, gain, shift):
    centre = jnp.mean(x, axis=-1, keepdims=True)
    away = x - centre
    spread = jnp.mean(away * away, axis=-1, keepdims=True)
    return (away * lax.rsqrt(spread + 1e-05) * gain + shift).astype(BF16)


def project(x_ref, gain, shift, w64, lsend, rsend):
    pieces = []
    for k in range(4):
        normed = standardize(x_ref[k].astype(F32), gain[...], shift[...])
        both = lax.dot_general(w64[...], normed, NT, preferred_element_type=F32)
        lsend[k * 32:(k + 1) * 32, :] = both[:32].astype(BF16)
        pieces.append(both[32:])
    for dc in range(4):
        rows = jnp.concatenate([p[dc * 8:(dc + 1) * 8] for p in pieces], axis=0).astype(BF16)
        for sl in range(2):
            rsend[dc, sl] = rows[:, sl * 128:(sl + 1) * 128]


def arrange_final(wfin, wide, w2t):
    wide[...] = wfin[...].astype(F32)
    for d2 in range(2):
        rows = jnp.concatenate([wide[pl.ds(dp * 2 + d2, 32, stride=32), :] for dp in range(16)], axis=0)
        turned = rows.T.astype(BF16)
        for dc in range(4):
            w2t[dc, d2 * 128:(d2 + 1) * 128, :] = turned[:, dc * 128:(dc + 1) * 128]


def outer_product(ib, pos, dc, lt, rt, outer):
    rows = pl.ds(pl.multiple_of(ib * 256, 256), 256)
    left = jnp.concatenate([lt[0, rows, :], lt[1, rows, :]], axis=1)
    right = jnp.concatenate([rt[sc, pl.ds(dc * 8, 8)].reshape(512, 128) for sc in range(4)], axis=1)
    p = lax.dot_general(left, right, NT, preferred_element_type=F32).astype(BF16)
    for i in range(8):
        for dp in range(4):
            outer[ib, (pos * 4 + dp) * 32:(pos * 4 + dp + 1) * 32, i * 128:(i + 1) * 128] = p[
                i * 32:(i + 1) * 32, dp * 128:(dp + 1) * 128
            ]


def last_product(ib, t, dcs, w2t, outer):
    weights = jnp.concatenate([w2t[dc] for dc in dcs], axis=1)
    res = jnp.dot(weights, outer[ib, t * 256:(t + 1) * 256, :], preferred_element_type=F32)
    lane = lax.broadcasted_iota(jnp.int32, (128, 1024), 1)
    return jnp.where(lane % 128 < 64, res[:128], res[128:])


def kernel(x_ref, gain, shift, w64, wfin, off, out,
           lt, rt, lsend, rsend, mid, stage, stage_f, wide, w2t, outer, partial,
           z_send, z_recv, f_send, x_send, x_recv, m_send, m_recv, s_send, s_recv, a_send, a_recv, b_send, b_recv, p_send, p_recv):
    q, ri, rj = lax.axis_index("seq"), lax.axis_index("ri"), lax.axis_index("rj")
    y, c, zl, xx = ri // 2, ri % 2, rj // 4, rj % 4
    half = zl // 2
    way = 1 - 2 * c
    self_z = half == q
    self_s = c == rj % 2
    self_s_count = jnp.where(self_s, 1, 0)

    def at_x(n):
        return (q, ri, zl * 4 + (xx + n + 4) % 4)

    def at_y(n):
        return (q, 2 * ((y + n + 8) % 8) + c, rj)

    def at_w(h, w):
        return (h, ri, (w + h * (3 - 2 * w)) * 4 + xx)

    peer = (q, 2 * y + 1 - c, rj)
    place = zl + q * (3 - 2 * zl)
    src = 4 * (q + half - 2 * q * half) + (zl % 2 + half - 2 * (zl % 2) * half)

    barrier = pltpu.get_barrier_semaphore()

    def greet(dev):
        pl.semaphore_signal(barrier, inc=1, device_id=dev, device_id_type=MESH)

    for s in range(16):
        for a in range(2):
            me = jnp.logical_and(self_s, jnp.logical_and(a == q, s == rj))

            @pl.when(jnp.logical_not(me))
            def _():
                greet((a, 2 * y + rj % 2, s))

    for n in (4, 3, -3, 2, -2, 1, -1):
        greet(at_y(n))

    def greet_place(w):
        @pl.when(w >= 0)
        def _():
            greet((jnp.where(w >= 4, 1 - q, q), ri, jnp.where(q == 0, w % 4, 3 - w % 4) * 4 + xx))

    def table(*values):
        v = values[3]
        for n in (2, 1, 0):
            v = jnp.where(place == n, values[n], v)
        return v

    greet_place(table(1, 0, 0, 1))
    greet_place(table(5, 4, 1, 4))
    greet_place(table(1, 0, 5, 2))
    greet_place(table(-1, -1, 3, 2))
    for n in (1, -1, 2):
        greet(at_x(n))
    greet(peer)

    project(x_ref, gain, shift, w64, lsend, rsend)

    z_targets = jnp.where(src == 1, 3, 2) + jnp.where(place == 2, 2, 1)
    pl.semaphore_wait(barrier, 32 - self_s_count + 7 + z_targets + 4)

    mid_slot = mid.at[y]

    def along_y(n):
        to = (y + n + 8) % 8
        return remote(rsend.at[to % 4], mid_slot, m_send.at[n % 8], m_recv.at[y], at_y(n))

    for n in (4, 3, -3, 2, -2, 1, -1):
        along_y(n).start()
    own_mid = pltpu.make_async_copy(rsend.at[y % 4], mid_slot, m_recv.at[y])
    own_mid.start()

    def left_slot(h, e, x):
        a = e // 2 + h - 2 * (e // 2) * h
        b = e % 2 + h - 2 * (e % 2) * h
        return lt.at[a, pl.ds(pl.multiple_of((b * 4 + x) * 128, 128), 128), :]

    own = src % 4 + 2 * (src // 4)
    z_slot = left_slot(half, own, xx)

    def z_copy(t):
        w = (1 - src % 2, jnp.where(src == 4, 3, 2), 3)[t]
        return remote(lsend, z_slot, z_send.at[t], z_recv.at[own], at_w(half, w))

    z_copy(1).start()

    @pl.when(src == 1)
    def _():
        z_copy(2).start()

    z_copy(0).start()

    @pl.when(self_z)
    def _():
        pltpu.make_async_copy(lsend, z_slot, z_recv.at[own]).start()

    def in_plane(n, sl, qd):
        ys = (y + n + 8) % 8
        dev = (qd, 2 * y + sl, 2 * ys + c)
        me = jnp.logical_and(jnp.logical_and(qd == q, sl == c), 2 * ys + c == rj)
        dst = stage.at[q, pl.ds(pl.multiple_of(rj * 32, 32), 32), :]
        sem = s_recv.at[q * 16 + rj]
        at = (n % 8) * 4 + sl * 2 + qd
        return me, remote(mid.at[ys, sl], dst, s_send.at[at], sem, dev), pltpu.make_async_copy(mid.at[ys, sl], dst, sem)

    hops = (0, 1, -1, 2, -2, 3, -3, 4)

    def spread(n):
        ys = (y + n + 8) % 8
        pltpu.make_async_copy(mid.at[ys], mid.at[ys], m_recv.at[ys]).wait()
        for sl in range(2):
            for qd in range(2):
                me, far, near = in_plane(n, sl, qd)

                @pl.when(me)
                def _():
                    near.start()

                @pl.when(jnp.logical_not(me))
                def _():
                    far.start()

    arrange_final(wfin, wide, w2t)

    order = [table(0, 1, 1, 2), table(1, 0, 0, 1), table(3, 2, 3, 0), table(2, 3, 2, 3)]
    passing = [place == 3, place == 2, place <= 2]

    straight = (3,)

    def onward(p):
        e = order[p]
        s = left_slot(q, e, xx)
        return remote(s, s, f_send.at[p], z_recv.at[e], at_w(q, place + 1 - 2 * (place % 2)))

    def x_copy(p, kind):
        e = order[p]
        if kind == 2 and p in straight:
            s, n = left_slot(q, e, xx), 2
        elif kind == 2:
            s, n = left_slot(q, e, (xx - way + 4) % 4), way
        else:
            s, n = left_slot(q, e, xx), (way, -way)[kind]
        return remote(s, s, x_send.at[e * 3 + kind], x_recv.at[e * 3 + kind], at_x(n))

    def x_land(p, kind):
        e = order[p]
        s = left_slot(q, e, (xx + (-way, way, 2)[kind] + 4) % 4)
        pltpu.make_async_copy(s, s, x_recv.at[e * 3 + kind]).wait()

    def z_land(p):
        e = order[p]
        s = left_slot(q, e, xx)
        pltpu.make_async_copy(s, s, z_recv.at[e]).wait()
        if p < 3:
            @pl.when(passing[p])
            def _():
                onward(p).start()
        x_copy(p, 0).start()
        x_copy(p, 1).start()
        if p in straight:
            x_copy(p, 2).start()

    def x_step(p):
        x_land(p, 0)
        if p not in straight:
            x_copy(p, 2).start()

    near_zl = (zl, zl + 1 - 2 * (zl % 2), (zl + 2) % 4, 3 - zl)
    parts = [(q, near_zl[n]) for n in (0, 1, 2, 3)] + [(1 - q, near_zl[n]) for n in (3, 2, 1, 0)]

    def part(step, g):
        a, z = parts[g]
        return rt.at[2 * a + c, pl.ds(((y + step + 8) % 4) * 8, 8), pl.ds(pl.multiple_of(z * 16, 16), 16), :]

    def quarter(step, a, core):
        return rt.at[2 * a + core, pl.ds(((y + step + 8) % 4) * 8, 8)]

    def ring_a(k, g):
        s = part(-way * k, g)
        return remote(s, s, a_send.at[k * 8 + g], a_recv.at[k * 8 + g], at_y(way))

    def ring_b(g):
        s = part(0, g)
        return remote(s, s, b_send.at[g], b_recv.at[g], at_y(-way))

    steps = (0, -1, 1, -2)

    def here(kind, n):
        a = parts[n * 4][0]
        s = quarter(way * steps[kind], a, c)
        return remote(s, s, p_send.at[kind * 2 + a], p_recv.at[kind * 2 + a], peer)

    def here_land(kind):
        for a in range(2):
            s = quarter(-way * steps[kind], a, 1 - c)
            pltpu.make_async_copy(s, s, p_recv.at[kind * 2 + a]).wait()

    def land(sem, s):
        pltpu.make_async_copy(s, s, sem).wait()

    def assemble(g):
        a, z = parts[g]
        for x in range(4):
            piece = stage.at[a, pl.ds(pl.multiple_of((z * 4 + x) * 32, 32), 32), :]
            land(s_recv.at[a * 16 + z * 4 + x], piece)
        stage_f[g] = stage[a, pl.ds(pl.multiple_of(z * 128, 128), 128), :].astype(F32)
        for d in range(8):
            rt[2 * a + c, (y % 4) * 8 + d, pl.ds(pl.multiple_of(z * 16, 16), 16), :] = stage_f[
                g, pl.ds(d, 16, stride=8), :
            ].astype(BF16)
        ring_a(0, g).start()
        ring_b(g).start()
        if g % 4 == 3:
            here(0, g // 4).start()

    def pass_on(g):
        land(a_recv.at[g], part(-way, g))
        ring_a(1, g).start()
        land(b_recv.at[g], part(way, g))
        if g % 4 == 3:
            here(1, g // 4).start()
            here(2, g // 4).start()

    spread(0)
    spread(1)
    spread(-1)
    z_land(0)
    spread(2)
    spread(-2)
    z_land(1)
    spread(3)
    spread(-3)
    spread(4)
    z_land(2)
    x_step(0)
    for g in range(0, 4):
        assemble(g)
    x_step(1)
    z_land(3)
    for g in range(4, 8):
        assemble(g)
    x_step(2)
    for g in range(0, 8):
        pass_on(g)
    x_step(3)
    for n in hops:
        if n:
            along_y(n).wait_send()
        for sl in range(2):
            for qd in range(2):
                me, far, near = in_plane(n, sl, qd)

                @pl.when(jnp.logical_not(me))
                def _():
                    far.wait_send()

    z_copy(0).wait_send()
    z_copy(1).wait_send()

    @pl.when(src == 1)
    def _():
        z_copy(2).wait_send()

    for p in range(3):
        @pl.when(passing[p])
        def _():
            onward(p).wait_send()
    for p in range(4):
        x_land(p, 1)
        x_land(p, 2)
    for kind in range(3):
        here_land(kind)

    dcs = [(y + n) % 4 for n in (0, 1, 3, 2)]

    for pos in range(3):
        for ib in range(4):
            outer_product(ib, pos, dcs[pos], lt, rt, outer)
    for ib in range(4):
        partial[ib] = last_product(ib, 0, dcs[:2], w2t, outer)

    for p in range(4):
        for kind in range(3):
            x_copy(p, kind).wait_send()
    for g in range(8):
        ring_a(0, g).wait_send()
        ring_b(g).wait_send()
    for kind in range(3):
        for n in range(2):
            here(kind, n).wait_send()

    for g in range(8):
        land(a_recv.at[8 + g], part(-way * 2, g))
        if g % 4 == 3:
            here(3, g // 4).start()
    here_land(3)

    scale = 1.0 / (2 * x_ref.shape[1])

    for ib in range(4):
        outer_product(ib, 3, dcs[3], lt, rt, outer)
    for ib in range(4):
        total = partial[ib] + last_product(ib, 1, dcs[2:], w2t, outer)
        for i in range(8):
            both = total[:, i * 128:(i + 1) * 128].T
            out[ib * 8 + i] = ((both[:64] + both[64:]) * scale + off[...]).astype(BF16)

    for g in range(8):
        ring_a(1, g).wait_send()
    for n in range(2):
        here(3, n).wait_send()


def per_device(embedding, gain, shift, projector, final, offset):
    dma = pltpu.SemaphoreType.DMA
    operands = (jnp.swapaxes(embedding, 0, 1), gain.reshape(1, -1), shift.reshape(1, -1), projector.T, final, offset.reshape(1, -1))
    return pl.pallas_call(
        kernel,
        out_shape=jax.ShapeDtypeStruct((32, 64, 128), BF16),
        in_specs=[pl.BlockSpec(memory_space=pltpu.VMEM)] * 6,
        out_specs=pl.BlockSpec(memory_space=pltpu.VMEM),
        scratch_shapes=[
            pltpu.VMEM((2, 1024, 256), BF16),
            pltpu.VMEM((4, 32, 64, 128), BF16),
            pltpu.VMEM((128, 256), BF16),
            pltpu.VMEM((4, 2, 32, 128), BF16),
            pltpu.VMEM((8, 2, 32, 128), BF16),
            pltpu.VMEM((2, 512, 128), BF16),
            pltpu.VMEM((8, 128, 128), F32),
            pltpu.VMEM((1024, 128), F32),
            pltpu.VMEM((4, 256, 128), BF16),
            pltpu.VMEM((4, 512, 1024), BF16),
            pltpu.VMEM((4, 128, 1024), F32),
            dma((3,)), dma((4,)), dma((3,)), dma((12,)), dma((12,)), dma((8,)), dma((8,)), dma((32,)), dma((32,)),
            dma((16,)), dma((16,)), dma((8,)), dma((8,)), dma((8,)), dma((8,)),
        ],
        compiler_params=pltpu.CompilerParams(
            collective_id=0, has_side_effects=True, vmem_limit_bytes=48 << 20
        ),
    )(*operands)


def solution(mesh):
    in_specs = (P("seq", ("ri", "rj"), None), P(), P(), P(), P(), P())
    return jax.shard_map(
        per_device, mesh=mesh, in_specs=in_specs, out_specs=P(("ri", "seq"), "rj", None), check_vma=False
    )
```
